32 devices in a mesh: member: 2 (over y), gx: 8 (over z, x), gy: 2 (over core).
Axes of the slice: x: 2, y: 2, z: 4, core: 2. Of those that a mesh axis runs over, the one named last changes fastest.
Arguments:
- conserved: float32 [5, 64, 64, 256], P(None, ('member', 'gx'), 'gy'), parts along dimension 1, may hold values from -3 to 18, as said below
- solid_mask: int32 [64, 64, 256], P(('member', 'gx'), 'gy'), parts along dimension 0, may hold values 0 or 1
- penalty: float32 [512], P('member'), parts along dimension 0, may hold values from 20 to 400
Outputs:
- advanced: float32 [5, 64, 64, 256], P(None, ('member', 'gx'), 'gy'), parts along dimension 1
The draws below stay inside these ranges and needn't reach their ends.
There are 2 independent parts, one for each index of `member`. The reference program is written for one: setup_inputs(seed, part) draws one part's arguments, and reference() takes and returns one part's arrays. A program takes and returns all parts, laid end to end along the dimension named above; each array names one. Nothing has to cross between parts.
Inputs may be any that keep to these rules, and one draw needn't show every extreme that they name: `conserved`: component 0 (density) lies in 0.8 to 2 and the pressure computed from every cell is positive.
All inputs are finite; a program needn't handle non-finite values. No bound on the sum of `solid_mask` on one device may be relied on, other than what follows from the above.
Results may differ from the reference program's by a relative error of at most 0.00002.
Values sent between devices are 32-bit elements; how exact they have to be, the bound alone decides.
A program may use at most 64 MiB of HBM per device.

```python
import math
import jax
import jax.numpy as jnp
from jax import lax

GRID_POINTS_X = 32
GRID_POINTS_Y = 64
GRID_POINTS_Z = 256


def draw_conserved(key, part):
    key = jax.random.fold_in(key, 11)
    generator_seeds = jax.random.split(key, 3)
    position = (jnp.arange(GRID_POINTS_X, dtype=jnp.float32) + 0.5) / GRID_POINTS_X
    ramp = position
    lowest = 0.2
    highest = 1.2
    perturbation_height = (lowest * (highest / lowest) ** ramp)[:, None, None]
    mass_per_volume = jax.random.uniform(generator_seeds[0], (GRID_POINTS_X, GRID_POINTS_Y, GRID_POINTS_Z), jnp.float32, 0.8, 2.0)
    thermal_state = 1.5 * perturbation_height * perturbation_height * jax.random.uniform(generator_seeds[1], (GRID_POINTS_X, GRID_POINTS_Y, GRID_POINTS_Z), jnp.float32, 0.5, 1.0)
    velocity = perturbation_height[None] * jax.random.uniform(generator_seeds[2], (3, GRID_POINTS_X, GRID_POINTS_Y, GRID_POINTS_Z), jnp.float32, -1.0, 1.0)
    normal_stress = mass_per_volume * thermal_state
    squares = velocity[0] * velocity[0] + velocity[1] * velocity[1] + velocity[2] * velocity[2]
    energy = normal_stress / 0.4 + 0.5 * mass_per_volume * squares
    momenta = mass_per_volume[None] * velocity
    return jnp.concatenate([mass_per_volume[None], momenta, energy[None]], 0).astype(jnp.float32)


def with_ends(array, rng, least, high):
    longest = array.shape.index(max(array.shape))
    spots = []
    for shift in (0, 1):
        where = [jax.random.randint(jax.random.fold_in(rng, axis), (), 0, length) for axis, length in enumerate(array.shape)]
        where[longest] = (where[longest] + shift) % array.shape[longest]
        spots.append(tuple(where))
    return array.at[spots[0]].set(least).at[spots[1]].set(high)


def setup_inputs(seed: int = 0, part: int = 0) -> dict:
    key_of = jax.random.split(jax.random.key(seed), 4)
    own_keys = jax.random.split(jax.random.fold_in(key_of[3], part), 4)
    conserved = draw_conserved(jax.random.fold_in(jax.random.fold_in(key_of[3], part), 71), part)
    solid_mask = with_ends((jax.random.randint(own_keys[1], (GRID_POINTS_X, GRID_POINTS_Y, GRID_POINTS_Z), 0, 3) < 1).astype(jnp.int32), jax.random.fold_in(own_keys[1], 1), 0, 1)
    penalty = jnp.clip(jnp.exp(jax.random.uniform(own_keys[2], (GRID_POINTS_Z,), jnp.float32, math.log(20.0), math.log(400.0))), 20.0, 400.0)
    return {"conserved": conserved, "solid_mask": solid_mask, "penalty": penalty}


GAMMA_LESS = 0.4
GAMMA_FULL = 1.4
COURANT = 0.3
VISCOSITY = 0.05

def pressure_of(fields):
    mass_per_volume = fields[0]
    squares = fields[1] * fields[1] + fields[2] * fields[2] + fields[3] * fields[3]
    return (GAMMA_LESS * (fields[4] - 0.5 * squares / mass_per_volume), squares)

def speeds(fields):
    normal_stress, squares = pressure_of(fields)
    mass_per_volume = fields[0]
    return jnp.sqrt(squares / mass_per_volume / mass_per_volume) + jnp.sqrt(GAMMA_FULL * normal_stress / mass_per_volume)

def fluxes(fields, direction):
    mass_per_volume = fields[0]
    normal_stress, squares = pressure_of(fields)
    velocity = fields[1 + direction] / mass_per_volume
    components = [fields[1 + direction], fields[1] * velocity, fields[2] * velocity, fields[3] * velocity, (fields[4] + normal_stress) * velocity]
    components[1 + direction] = components[1 + direction] + normal_stress
    return jnp.stack(components)

def axis_slope(values, along, extent):
    first_part = lax.slice_in_dim(values, 0, extent, axis=along)
    second_part = lax.slice_in_dim(values, 1, extent + 1, axis=along)
    fourth_part = lax.slice_in_dim(values, 3, extent + 3, axis=along)
    fifth_part = lax.slice_in_dim(values, 4, extent + 4, axis=along)
    return (first_part - 8.0 * second_part + 8.0 * fourth_part - fifth_part) / 12.0

def axis_curve(values, along, extent):
    first_part = lax.slice_in_dim(values, 0, extent, axis=along)
    second_part = lax.slice_in_dim(values, 1, extent + 1, axis=along)
    middle_part = lax.slice_in_dim(values, 2, extent + 2, axis=along)
    fourth_part = lax.slice_in_dim(values, 3, extent + 3, axis=along)
    fifth_part = lax.slice_in_dim(values, 4, extent + 4, axis=along)
    return (-first_part + 16.0 * second_part - 30.0 * middle_part + 16.0 * fourth_part - fifth_part) / 12.0

def roll_slope(values):
    return (jnp.roll(values, 2, 3) - 8.0 * jnp.roll(values, 1, 3) + 8.0 * jnp.roll(values, -1, 3) - jnp.roll(values, -2, 3)) / 12.0

def roll_curve(values):
    return (-jnp.roll(values, 2, 3) + 16.0 * jnp.roll(values, 1, 3) - 30.0 * values + 16.0 * jnp.roll(values, -1, 3) - jnp.roll(values, -2, 3)) / 12.0

def operate(padded):
    extent_x = padded.shape[1] - 4
    extent_y = padded.shape[2] - 4
    inner_cells = padded[:, 2:-2, 2:-2]
    strip_x = padded[:, :, 2:-2]
    strip_y = padded[:, 2:-2, :]
    divergence = axis_slope(fluxes(strip_x, 0), 1, extent_x)
    divergence = divergence + axis_slope(fluxes(strip_y, 1), 2, extent_y)
    divergence = divergence + roll_slope(fluxes(inner_cells, 2))
    diffusion = axis_curve(strip_x[1:], 1, extent_x) + axis_curve(strip_y[1:], 2, extent_y) + roll_curve(inner_cells[1:])
    return jnp.concatenate([-divergence[:1], -divergence[1:] + VISCOSITY * diffusion], 0)

def damp_momenta(fields, time_step, brinkman):
    return jnp.concatenate([fields[:1], fields[1:4] / (1.0 + time_step * brinkman), fields[4:]], 0)

def wrap_pad(fields):
    return jnp.pad(fields, ((0, 0), (2, 2), (2, 2), (0, 0)), mode='wrap')

def reference(conserved, solid_mask, penalty):
    brinkman = solid_mask.astype(jnp.float32) * penalty[None, None, :]
    time_step = COURANT / jnp.max(speeds(conserved))
    section_one = damp_momenta(conserved + time_step * operate(wrap_pad(conserved)), time_step, brinkman)
    section_two = 0.5 * conserved + 0.5 * (section_one + time_step * operate(wrap_pad(section_one)))
    return damp_momenta(section_two, time_step, brinkman)
```

```python
import functools

import jax
import jax.numpy as jnp
from jax import lax
from jax.experimental import pallas as pl
from jax.experimental.pallas import tpu as pltpu
from jax.sharding import PartitionSpec as P

GAMMA_LESS = 0.4
GAMMA_FULL = 1.4
COURANT = 0.3
VISCOSITY = 0.05
MESH = pl.DeviceIdType.MESH
EDGE = 8


def rolled(value, shift, axis):
    return pltpu.roll(value, shift % value.shape[axis], axis)


def primitives(read):
    rho, m0, m1, m2, energy = [read(c) for c in range(5)]
    inverse = 1.0 / rho
    squares = m0 * m0 + m1 * m1 + m2 * m2
    pressure = GAMMA_LESS * (energy - 0.5 * squares * inverse)
    return rho, (m0, m1, m2), energy, inverse, squares, pressure


def flux(momenta, energy, inverse, pressure, k):
    w = momenta[k] * inverse
    parts = [momenta[k]] + [m * w for m in momenta] + [(energy + pressure) * w]
    parts[1 + k] = parts[1 + k] + pressure
    return parts


def rolled_terms(f, q, axis):
    if q is None:
        return (
            8.0 * (rolled(f, 1, axis) - rolled(f, -1, axis))
            - (rolled(f, 2, axis) - rolled(f, -2, axis))
        )
    s = VISCOSITY * q
    big, wide = 8.0 * f, 16.0 * s
    return (
        rolled(wide + big, 1, axis)
        + rolled(wide - big, -1, axis)
        - rolled(s + f, 2, axis)
        - rolled(s - f, -2, axis)
    )


def kernel(n, q_hbm, mask_hbm, penalty, out, state, mask, fluxes, stage, best,
           local_sem, sx, rx, sz, rz, sy, ry, sm, rm):
    i = lax.axis_index("gx")
    g = lax.axis_index("gy")
    layers, rows, width = q_hbm.shape[1:]
    lo, hi, tall = EDGE, EDGE + rows, rows + 2 * EDGE
    half = layers // 2
    parity = lax.rem(i, 2)
    partner = i + 1 - 2 * parity
    sibling = 1 - g
    z_to = lax.rem(i + 2 - 4 * parity + n, n)
    z_from = lax.rem(i - 2 + 4 * parity + n, n)
    steps = n.bit_length() - 1
    flips = [i + (1 << k) * (1 - 2 * lax.rem(i // (1 << k), 2)) for k in range(steps)]

    local_q = pltpu.make_async_copy(
        q_hbm, state.at[:, layers:2 * layers, lo:hi, :], local_sem.at[0])
    local_m = pltpu.make_async_copy(
        mask_hbm, mask.at[layers:2 * layers, lo:hi, :], local_sem.at[1])
    local_q.start()
    local_m.start()

    barrier = pltpu.get_barrier_semaphore()
    others = [partner, z_to, z_from] + flips[1:]
    for j in others:
        pl.semaphore_signal(barrier, inc=1, device_id={"gx": j}, device_id_type=MESH)
    pl.semaphore_signal(barrier, inc=1, device_id={"gy": sibling}, device_id_type=MESH)
    pl.semaphore_wait(barrier, len(others) + 1)

    def remote(src, dst, send, recv, where):
        return pltpu.make_async_remote_copy(
            src_ref=src, dst_ref=dst, send_sem=send, recv_sem=recv,
            device_id=where, device_id_type=MESH)

    own = (half * parity, half - half * parity)
    seen = (half - half * parity, half * parity)
    x_out, x_in = 2 * layers * parity, 2 * layers * (1 - parity)
    z_out = z_in = 2 * layers * parity
    pieces = [(h, c) for h in range(2) for c in range(-1, 5)]
    x_sends, x_waits, z_sends, z_waits = [], [], [], []
    for k, (h, c) in enumerate(pieces):
        def x_copy(start, where):
            if c < 0:
                return remote(
                    mask_hbm.at[pl.ds(start, half)],
                    mask.at[pl.ds(where + start, half), lo:hi, :],
                    sx.at[k], rx.at[k], {"gx": partner})
            return remote(
                q_hbm.at[c, pl.ds(start, half)],
                state.at[c, pl.ds(where + start, half), lo:hi, :],
                sx.at[k], rx.at[k], {"gx": partner})

        def z_copy(start, source, target):
            if c < 0:
                return remote(
                    mask.at[pl.ds(source + start, half), lo:hi, :],
                    mask.at[pl.ds(target + start, half), lo:hi, :],
                    sz.at[k], rz.at[k], {"gx": z_to})
            return remote(
                state.at[c, pl.ds(source + start, half), lo:hi, :],
                state.at[c, pl.ds(target + start, half), lo:hi, :],
                sz.at[k], rz.at[k], {"gx": z_to})

        x_sends.append(x_copy(own[h], x_out))
        x_waits.append(x_copy(seen[h], x_in))
        if c < 0 and h == 1:
            z_sends.append(None)
            z_waits.append(None)
        else:
            z_sends.append(z_copy(seen[h], x_in, z_out))
            z_waits.append(z_copy(seen[h], z_in, z_in))

    for copy in x_sends:
        copy.start()

    to_sibling = {"gy": sibling}
    edges = [
        remote(q_hbm.at[:, :, 0:EDGE, :], state.at[:, layers:2 * layers, hi:tall, :],
               sy.at[0], ry.at[0], to_sibling),
        remote(q_hbm.at[:, :, rows - EDGE:rows, :], state.at[:, layers:2 * layers, 0:lo, :],
               sy.at[1], ry.at[1], to_sibling),
        remote(mask_hbm.at[:, 0:EDGE, :], mask.at[layers:2 * layers, hi:tall, :],
               sy.at[2], ry.at[2], to_sibling),
        remote(mask_hbm.at[:, rows - EDGE:rows, :], mask.at[layers:2 * layers, 0:lo, :],
               sy.at[3], ry.at[3], to_sibling),
    ]

    def corner(where, k):
        spot = pl.ds(where, half)
        return [
            remote(state.at[:, spot, lo:lo + EDGE, :], state.at[:, spot, hi:tall, :],
                   sy.at[k], ry.at[k], to_sibling),
            remote(state.at[:, spot, hi - EDGE:hi, :], state.at[:, spot, 0:lo, :],
                   sy.at[k + 1], ry.at[k + 1], to_sibling),
        ]

    corner_z = corner(z_in + seen[0], 4)
    corner_x = corner(x_in + seen[1], 6)
    for copy in edges:
        copy.start()
    local_q.wait()

    def speed_step(l, top):
        rho, _, _, inverse, squares, pressure = primitives(
            lambda c: state[c, layers + l, lo:hi, :])
        speed = jnp.sqrt(squares * inverse * inverse) + jnp.sqrt(
            GAMMA_FULL * pressure * inverse)
        for r in range(0, rows, 8):
            for z in range(0, width, 128):
                top = jnp.maximum(top, speed[r:r + 8, z:z + 128])
        return top

    best[0] = lax.fori_loop(0, layers, speed_step, jnp.zeros((8, 128), jnp.float32))

    def max_copy(k):
        where = {"gy": sibling} if k == 0 else {"gx": flips[k - 1]}
        return remote(best.at[2 * k], best.at[2 * k + 1], sm.at[k], rm.at[k], where)

    def max_finish(k):
        max_copies[k].wait_recv()
        best[2 * k + 2] = jnp.maximum(best[2 * k], best[2 * k + 1])

    max_copies = [max_copy(k) for k in range(steps + 1)]
    max_copies[0].start()
    done = 0
    for k, (h, c) in enumerate(pieces):
        x_waits[k].wait_recv()
        if z_sends[k] is not None:
            z_sends[k].start()
        if done <= steps and k >= 1:
            max_finish(done)
            done += 1
            if done <= steps:
                max_copies[done].start()
    for copy in corner_x:
        copy.start()
    for k in range(6):
        z_waits[k].wait_recv()
    for copy in corner_z:
        copy.start()
    while done <= steps:
        max_finish(done)
        done += 1
        if done <= steps:
            max_copies[done].start()
    for k in range(6, 12):
        if z_waits[k] is not None:
            z_waits[k].wait_recv()
    local_m.wait()
    for copy in edges + corner_x + corner_z:
        copy.wait_recv()

    top = jnp.max(best[2 * steps + 2], axis=1, keepdims=True)
    time_step = COURANT / jnp.max(top, axis=0, keepdims=True)
    scale = time_step / 12.0
    rates = penalty[...]

    def store_flux(source, first, last):
        def store(l, carry):
            _, momenta, energy, inverse, _, pressure = primitives(
                lambda c: source[c, l, first:last, :])
            parts = flux(momenta, energy, inverse, pressure, 0)
            for c in range(1, 5):
                fluxes[c - 1, l, first:last, :] = parts[c]
            return carry
        return store

    def change(source, l, first, last):
        _, momenta, energy, inverse, _, pressure = primitives(lambda c: source[c, l])
        fy = flux(momenta, energy, inverse, pressure, 1)
        inner = slice(first, last)
        fz = flux([m[inner] for m in momenta], energy[inner], inverse[inner], pressure[inner], 2)
        results = []
        for c in range(5):
            q = None if c == 0 else source[c, l]
            total = rolled_terms(fy[c], q, 0)[inner]
            if c == 0:
                total = total + rolled_terms(fz[c], None, 1)
                near = lambda d: source[1, l + d, first:last, :]
            else:
                total = total + rolled_terms(fz[c], q[inner], 1)
                near = lambda d: fluxes[c - 1, l + d, first:last, :]
            total = total + 8.0 * (near(-1) - near(1)) - (near(-2) - near(2))
            if c > 0:
                beside = lambda d: source[c, l + d, first:last, :]
                total = total + VISCOSITY * (
                    16.0 * (beside(-1) + beside(1)) - (beside(-2) + beside(2)) - 90.0 * q[inner])
            results.append(total)
        return results

    def damping(l, first, last):
        brinkman = mask[l, first:last, :].astype(jnp.float32) * rates
        return 1.0 / (1.0 + time_step * brinkman)

    def section_one(first, last):
        def body(l, carry):
            damp = damping(l, first, last)
            for c, total in enumerate(change(state, l, first, last)):
                value = state[c, l, first:last, :] + scale * total
                stage[c, l, first:last, :] = value * damp if 1 <= c <= 3 else value
            return carry
        return body

    near, far = layers - half, 2 * layers + half
    lax.fori_loop(0, near, store_flux(state, lo, hi), 0)
    lax.fori_loop(near, far, store_flux(state, 0, tall), 0)
    lax.fori_loop(far, 3 * layers, store_flux(state, lo, hi), 0)
    lax.fori_loop(near, layers, section_one(lo, hi), 0)
    lax.fori_loop(layers, 2 * layers, section_one(0, tall), 0)
    lax.fori_loop(2 * layers, far, section_one(lo, hi), 0)

    lax.fori_loop(near, far, store_flux(stage, lo, hi), 0)

    def section_two(t, carry):
        l = layers + t
        damp = damping(l, lo, hi)
        for c, total in enumerate(change(stage, l, lo, hi)):
            value = 0.5 * state[c, l, lo:hi, :] + 0.5 * (
                stage[c, l, lo:hi, :] + scale * total)
            out[c, t] = value * damp if 1 <= c <= 3 else value
        return carry

    lax.fori_loop(0, layers, section_two, 0)

    for copy in x_sends + edges + corner_x + corner_z + max_copies:
        copy.wait_send()
    for copy in z_sends:
        if copy is not None:
            copy.wait_send()


def per_device(n, conserved, solid_mask, penalty):
    _, layers, rows, width = conserved.shape
    tall = rows + 2 * EDGE
    steps = n.bit_length() - 1
    dma = pltpu.SemaphoreType.DMA
    return pl.pallas_call(
        functools.partial(kernel, n),
        out_shape=jax.ShapeDtypeStruct(conserved.shape, jnp.float32),
        in_specs=[
            pl.BlockSpec(memory_space=pl.ANY),
            pl.BlockSpec(memory_space=pl.ANY),
            pl.BlockSpec(memory_space=pltpu.VMEM),
        ],
        out_specs=pl.BlockSpec(memory_space=pltpu.VMEM),
        scratch_shapes=[
            pltpu.VMEM((5, 3 * layers, tall, width), jnp.float32),
            pltpu.VMEM((3 * layers, tall, width), jnp.int32),
            pltpu.VMEM((4, 3 * layers, tall, width), jnp.float32),
            pltpu.VMEM((5, 3 * layers, tall, width), jnp.float32),
            pltpu.VMEM((2 * steps + 3, 8, 128), jnp.float32),
            dma((2,)),
            dma((12,)), dma((12,)),
            dma((12,)), dma((12,)),
            dma((8,)), dma((8,)),
            dma((steps + 1,)), dma((steps + 1,)),
        ],
        compiler_params=pltpu.CompilerParams(
            collective_id=0, has_side_effects=True, vmem_limit_bytes=40 * 1024 * 1024),
    )(conserved, solid_mask, penalty.reshape(1, width))


def solution(mesh):
    return jax.shard_map(
        functools.partial(per_device, mesh.shape["gx"]),
        mesh=mesh,
        in_specs=(
            P(None, ("member", "gx"), "gy", None),
            P(("member", "gx"), "gy", None),
            P("member"),
        ),
        out_specs=P(None, ("member", "gx"), "gy", None),
        check_vma=False,
    )
```

```python
import functools

import jax
import jax.numpy as jnp
from jax import lax
from jax.experimental import pallas as pl
from jax.experimental.pallas import tpu as pltpu
from jax.sharding import PartitionSpec as P

GAMMA_LESS = 0.4
GAMMA_FULL = 1.4
COURANT = 0.3
VISCOSITY = 0.05
MESH = pl.DeviceIdType.MESH
EDGE = 8
AHEAD = 4


def rolled(value, shift, axis):
    return pltpu.roll(value, shift % value.shape[axis], axis)


def primitives(read):
    rho, m0, m1, m2, energy = [read(c) for c in range(5)]
    inverse = 1.0 / rho
    squares = m0 * m0 + m1 * m1 + m2 * m2
    pressure = GAMMA_LESS * (energy - 0.5 * squares * inverse)
    return rho, (m0, m1, m2), energy, inverse, squares, pressure


def flux(momenta, energy, inverse, pressure, k):
    w = momenta[k] * inverse
    parts = [momenta[k]] + [m * w for m in momenta] + [(energy + pressure) * w]
    parts[1 + k] = parts[1 + k] + pressure
    return parts


def rolled_terms(f, q, axis):
    if q is None:
        return (
            8.0 * (rolled(f, 1, axis) - rolled(f, -1, axis))
            - (rolled(f, 2, axis) - rolled(f, -2, axis))
        )
    s = VISCOSITY * q
    big, wide = 8.0 * f, 16.0 * s
    return (
        rolled(wide + big, 1, axis)
        + rolled(wide - big, -1, axis)
        - rolled(s + f, 2, axis)
        - rolled(s - f, -2, axis)
    )


def kernel(n, q_hbm, mask_hbm, penalty, out, state, mask, fluxes, fluxes_two, stage, part, best,
           local_sem, sx, rx, sz, rz, sy, ry, sm, rm):
    i = lax.axis_index("gx")
    g = lax.axis_index("gy")
    layers, rows, width = q_hbm.shape[1:]
    lo, hi, tall = EDGE, EDGE + rows, rows + 2 * EDGE
    half = layers // 2
    parity = lax.rem(i, 2)
    partner = i + 1 - 2 * parity
    sibling = 1 - g
    z_to = lax.rem(i + 2 - 4 * parity + n, n)
    z_from = lax.rem(i - 2 + 4 * parity + n, n)
    level = [lax.rem(i + 2 * m, n) for m in range(1, n // 2)]

    local_q = pltpu.make_async_copy(
        q_hbm, state.at[:, layers:2 * layers, lo:hi, :], local_sem.at[0])
    local_m = pltpu.make_async_copy(
        mask_hbm, mask.at[layers:2 * layers, lo:hi, :], local_sem.at[1])
    local_q.start()
    local_m.start()

    barrier = pltpu.get_barrier_semaphore()
    near_by = [{"gy": sibling}, {"gx": partner}, {"gx": partner, "gy": sibling}]
    others = near_by + [{"gx": j} for j in level]
    for where in others:
        pl.semaphore_signal(barrier, inc=1, device_id=where, device_id_type=MESH)
    pl.semaphore_wait(barrier, len(others))

    def remote(src, dst, send, recv, where):
        return pltpu.make_async_remote_copy(
            src_ref=src, dst_ref=dst, send_sem=send, recv_sem=recv,
            device_id=where, device_id_type=MESH)

    own = (half * parity, half - half * parity)
    seen = (half - half * parity, half * parity)
    x_out, x_in = 2 * layers * parity, 2 * layers * (1 - parity)
    z_out = z_in = 2 * layers * parity
    pieces = [(h, c) for h in range(2) for c in range(-1, 5)]
    x_sends, x_waits, z_sends, z_waits = [], [], [], []
    for k, (h, c) in enumerate(pieces):
        def x_copy(start, where):
            if c < 0:
                return remote(
                    mask_hbm.at[pl.ds(start, half)],
                    mask.at[pl.ds(where + start, half), lo:hi, :],
                    sx.at[k], rx.at[k], {"gx": partner})
            return remote(
                q_hbm.at[c, pl.ds(start, half)],
                state.at[c, pl.ds(where + start, half), lo:hi, :],
                sx.at[k], rx.at[k], {"gx": partner})

        def z_copy(start, source, target):
            if c < 0:
                return remote(
                    mask.at[pl.ds(source + start, half), lo:hi, :],
                    mask.at[pl.ds(target + start, half), lo:hi, :],
                    sz.at[k], rz.at[k], {"gx": z_to})
            return remote(
                state.at[c, pl.ds(source + start, half), lo:hi, :],
                state.at[c, pl.ds(target + start, half), lo:hi, :],
                sz.at[k], rz.at[k], {"gx": z_to})

        x_sends.append(x_copy(own[h], x_out))
        x_waits.append(x_copy(seen[h], x_in))
        if c < 0 and h == 1:
            z_sends.append(None)
            z_waits.append(None)
        else:
            z_sends.append(z_copy(seen[h], x_in, z_out))
            z_waits.append(z_copy(seen[h], z_in, z_in))

    for copy in x_sends[:AHEAD]:
        copy.start()

    to_sibling = {"gy": sibling}
    edges = [
        remote(q_hbm.at[:, :, 0:EDGE, :], state.at[:, layers:2 * layers, hi:tall, :],
               sy.at[0], ry.at[0], to_sibling),
        remote(q_hbm.at[:, :, rows - EDGE:rows, :], state.at[:, layers:2 * layers, 0:lo, :],
               sy.at[1], ry.at[1], to_sibling),
        remote(mask_hbm.at[:, 0:EDGE, :], mask.at[layers:2 * layers, hi:tall, :],
               sy.at[2], ry.at[2], to_sibling),
        remote(mask_hbm.at[:, rows - EDGE:rows, :], mask.at[layers:2 * layers, 0:lo, :],
               sy.at[3], ry.at[3], to_sibling),
    ]

    def corner(where, k):
        spot = pl.ds(where, half)
        return [
            remote(state.at[:, spot, lo:lo + EDGE, :], state.at[:, spot, hi:tall, :],
                   sy.at[k], ry.at[k], to_sibling),
            remote(state.at[:, spot, hi - EDGE:hi, :], state.at[:, spot, 0:lo, :],
                   sy.at[k + 1], ry.at[k + 1], to_sibling),
        ]

    corner_z = corner(z_in + seen[0], 4)
    corner_x = corner(x_in + seen[1], 6)
    for copy in edges:
        copy.start()
    local_q.wait()

    def speed_step(l, top):
        rho, _, _, inverse, squares, pressure = primitives(
            lambda c: state[c, layers + l, lo:hi, :])
        speed = jnp.sqrt(squares * inverse * inverse) + jnp.sqrt(
            GAMMA_FULL * pressure * inverse)
        for r in range(0, rows, 8):
            for z in range(0, width, 128):
                top = jnp.maximum(top, speed[r:r + 8, z:z + 128])
        return top

    best[0] = lax.fori_loop(0, layers, speed_step, jnp.zeros((8, 128), jnp.float32))

    def max_copy(k):
        source = 0 if k < 3 else 4
        return remote(best.at[source], best.at[k + 1 if k < 3 else k + 2],
                      sm.at[k], rm.at[k], others[k])

    max_copies = [max_copy(k) for k in range(len(others))]
    for copy in max_copies[:3]:
        copy.start()

    z_inner, z_outer = z_in + seen[0], z_in + seen[1]
    x_outer, x_inner = x_in + seen[0], x_in + seen[1]
    own_z = layers + half * parity
    own_x = layers + half * (1 - parity)

    def each(start, count, body):
        def step(t, carry):
            body(start + t)
            return carry
        lax.fori_loop(0, count, step, 0)

    def store_flux(source, first, last):
        target = fluxes if source is state else fluxes_two

        def store(l):
            _, momenta, energy, inverse, _, pressure = primitives(
                lambda c: source[c, l, first:last, :])
            parts = flux(momenta, energy, inverse, pressure, 0)
            for c in range(1, 5):
                target[c - 1, l, first:last, :] = parts[c]
        return store

    def store_part(source, first, last):
        inner = slice(first, last)

        def store(l):
            _, momenta, energy, inverse, _, pressure = primitives(lambda c: source[c, l])
            fy = flux(momenta, energy, inverse, pressure, 1)
            fz = flux(
                [m[inner] for m in momenta], energy[inner], inverse[inner], pressure[inner], 2)
            for c in range(5):
                q = None if c == 0 else source[c, l]
                total = rolled_terms(fy[c], q, 0)[inner]
                if c == 0:
                    total = total + rolled_terms(fz[c], None, 1)
                else:
                    total = total + rolled_terms(fz[c], q[inner], 1)
                    total = total - (90.0 * VISCOSITY) * q[inner]
                part[c, l, first:last, :] = total
        return store

    def whole(source, c, l, first, last):
        at = lambda ref, index, d: ref[index, l + d, first:last, :]
        x_flux = fluxes if source is state else fluxes_two
        f = (lambda d: at(source, 1, d)) if c == 0 else (lambda d: at(x_flux, c - 1, d))
        total = part[c, l, first:last, :] + 8.0 * (f(-1) - f(1)) - (f(-2) - f(2))
        if c > 0:
            q = lambda d: at(source, c, d)
            total = total + VISCOSITY * (16.0 * (q(-1) + q(1)) - (q(-2) + q(2)))
        return total

    def damping(l, first, last, time_step):
        brinkman = mask[l, first:last, :].astype(jnp.float32) * penalty[...]
        return 1.0 / (1.0 + time_step * brinkman)

    def section_one(first, last, time_step):
        scale = time_step / 12.0

        def body(l):
            damp = damping(l, first, last, time_step)
            for c in range(5):
                value = state[c, l, first:last, :] + scale * whole(state, c, l, first, last)
                stage[c, l, first:last, :] = value * damp if 1 <= c <= 3 else value
        return body

    for k in range(len(pieces)):
        x_waits[k].wait_recv()
        if z_sends[k] is not None:
            z_sends[k].start()
        if k + AHEAD < len(pieces):
            x_sends[k + AHEAD].start()
        if k == 1:
            for copy in max_copies[:3]:
                copy.wait_recv()
            best[4] = jnp.maximum(
                jnp.maximum(best[0], best[1]), jnp.maximum(best[2], best[3]))
            for copy in max_copies[3:]:
                copy.start()
            for copy in edges:
                copy.wait_recv()
            each(own_z, half, store_part(state, 0, tall))
        if k == 2:
            each(own_x, half, store_part(state, 0, tall))
        if k == 3:
            each(layers, layers, store_flux(state, 0, tall))
        if k == 5:
            each(x_outer, half, store_flux(state, lo, hi))
        if k == 7:
            for h in range(6):
                z_waits[h].wait_recv()
            for copy in corner_z:
                copy.start()
            for copy in max_copies[3:]:
                copy.wait_recv()
        if k == 8:
            for copy in corner_z:
                copy.wait_recv()
            each(z_inner, half, store_flux(state, 0, tall))
            each(z_inner, half, store_part(state, lo, hi))
        if k == 9:
            local_m.wait()
            top = best[4]
            for m in range(len(level)):
                top = jnp.maximum(top, best[5 + m])
            top = jnp.max(jnp.max(top, axis=1, keepdims=True), axis=0, keepdims=True)
            time_step = COURANT / top
            each(own_z, half, section_one(0, tall, time_step))
        if k == 10:
            each(own_z, half, store_part(stage, lo, hi))
            each(own_z, half, store_flux(stage, lo, hi))

    for copy in corner_x:
        copy.start()
    each(x_inner, half, store_flux(state, lo, hi))
    each(own_x, half, section_one(lo, hi, time_step))
    for k in range(7, 12):
        z_waits[k].wait_recv()
    each(z_outer, half, store_flux(state, lo, hi))
    each(z_inner, half, section_one(lo, hi, time_step))
    each(z_inner, half, store_flux(stage, lo, hi))
    for copy in corner_x:
        copy.wait_recv()
    for first, last in ((0, lo), (hi, tall)):
        each(x_inner, half, store_flux(state, first, last))
        each(own_x, half, section_one(first, last, time_step))
    each(x_inner, half, store_part(state, lo, hi))
    each(x_inner, half, section_one(lo, hi, time_step))
    each(x_inner, half, store_flux(stage, lo, hi))
    each(own_x, half, store_part(stage, lo, hi))
    each(own_x, half, store_flux(stage, lo, hi))

    scale = time_step / 12.0

    def section_two(l):
        damp = damping(l, lo, hi, time_step)
        for c in range(5):
            value = 0.5 * state[c, l, lo:hi, :] + 0.5 * (
                stage[c, l, lo:hi, :] + scale * whole(stage, c, l, lo, hi))
            out[c, l - layers] = value * damp if 1 <= c <= 3 else value

    each(layers, layers, section_two)

    for copy in x_sends + edges + corner_x + corner_z + max_copies:
        copy.wait_send()
    for copy in z_sends:
        if copy is not None:
            copy.wait_send()


def per_device(n, conserved, solid_mask, penalty):
    _, layers, rows, width = conserved.shape
    tall = rows + 2 * EDGE
    dma = pltpu.SemaphoreType.DMA
    return pl.pallas_call(
        functools.partial(kernel, n),
        out_shape=jax.ShapeDtypeStruct(conserved.shape, jnp.float32),
        in_specs=[
            pl.BlockSpec(memory_space=pl.ANY),
            pl.BlockSpec(memory_space=pl.ANY),
            pl.BlockSpec(memory_space=pltpu.VMEM),
        ],
        out_specs=pl.BlockSpec(memory_space=pltpu.VMEM),
        scratch_shapes=[
            pltpu.VMEM((5, 3 * layers, tall, width), jnp.float32),
            pltpu.VMEM((3 * layers, tall, width), jnp.int32),
            pltpu.VMEM((4, 3 * layers, tall, width), jnp.float32),
            pltpu.VMEM((4, 3 * layers, tall, width), jnp.float32),
            pltpu.VMEM((5, 3 * layers, tall, width), jnp.float32),
            pltpu.VMEM((5, 3 * layers, tall, width), jnp.float32),
            pltpu.VMEM((n // 2 + 4, 8, 128), jnp.float32),
            dma((2,)),
            dma((12,)), dma((12,)),
            dma((12,)), dma((12,)),
            dma((8,)), dma((8,)),
            dma((n // 2 + 2,)), dma((n // 2 + 2,)),
        ],
        compiler_params=pltpu.CompilerParams(
            collective_id=0, has_side_effects=True, vmem_limit_bytes=40 * 1024 * 1024),
    )(conserved, solid_mask, penalty.reshape(1, width))


def solution(mesh):
    return jax.shard_map(
        functools.partial(per_device, mesh.shape["gx"]),
        mesh=mesh,
        in_specs=(
            P(None, ("member", "gx"), "gy", None),
            P(("member", "gx"), "gy", None),
            P("member"),
        ),
        out_specs=P(None, ("member", "gx"), "gy", None),
        check_vma=False,
    )
```

```python
import functools

import jax
import jax.numpy as jnp
from jax import lax
from jax.experimental import pallas as pl
from jax.experimental.pallas import tpu as pltpu
from jax.sharding import PartitionSpec as P

GAMMA_LESS = 0.4
GAMMA_FULL = 1.4
COURANT = 0.3
VISCOSITY = 0.05
MESH = pl.DeviceIdType.MESH
EDGE = 8
AHEAD = 4


def rolled(value, shift, axis):
    return pltpu.roll(value, shift % value.shape[axis], axis)


def primitives(read):
    rho, m0, m1, m2, energy = [read(c) for c in range(5)]
    inverse = 1.0 / rho
    squares = m0 * m0 + m1 * m1 + m2 * m2
    pressure = GAMMA_LESS * (energy - 0.5 * squares * inverse)
    return rho, (m0, m1, m2), energy, inverse, squares, pressure


def flux(momenta, energy, inverse, pressure, k):
    w = momenta[k] * inverse
    parts = [momenta[k]] + [m * w for m in momenta] + [(energy + pressure) * w]
    parts[1 + k] = parts[1 + k] + pressure
    return parts


def rolled_terms(f, q, axis):
    if q is None:
        return (
            8.0 * (rolled(f, 1, axis) - rolled(f, -1, axis))
            - (rolled(f, 2, axis) - rolled(f, -2, axis))
        )
    s = VISCOSITY * q
    big, wide = 8.0 * f, 16.0 * s
    return (
        rolled(wide + big, 1, axis)
        + rolled(wide - big, -1, axis)
        - rolled(s + f, 2, axis)
        - rolled(s - f, -2, axis)
    )


def kernel(n, q_own, mask_own, penalty, out, state, mask, fluxes, fluxes_two, stage, part, best,
           local_sem, sx, rx, sz, rz, sy, ry, sm, rm):
    i = lax.axis_index("gx")
    g = lax.axis_index("gy")
    layers, rows, width = q_own.shape[1:]
    lo, hi, tall = EDGE, EDGE + rows, rows + 2 * EDGE
    half = layers // 2
    parity = lax.rem(i, 2)
    partner = i + 1 - 2 * parity
    sibling = 1 - g
    z_to = lax.rem(i + 2 - 4 * parity + n, n)
    z_from = lax.rem(i - 2 + 4 * parity + n, n)
    level = [lax.rem(i + 2 * m, n) for m in range(1, n // 2)]

    barrier = pltpu.get_barrier_semaphore()
    near_by = [{"gy": sibling}, {"gx": partner}, {"gx": partner, "gy": sibling}]
    others = near_by + [{"gx": j} for j in level]
    for where in others:
        pl.semaphore_signal(barrier, inc=1, device_id=where, device_id_type=MESH)
    local_q = pltpu.make_async_copy(
        q_own, state.at[:, layers:2 * layers, lo:hi, :], local_sem.at[0])
    local_m = pltpu.make_async_copy(
        mask_own, mask.at[layers:2 * layers, lo:hi, :], local_sem.at[1])
    local_q.start()
    local_m.start()

    def speed_step(l, top):
        rho, _, _, inverse, squares, pressure = primitives(
            lambda c: q_own[c, l])
        speed = jnp.sqrt(squares * inverse * inverse) + jnp.sqrt(
            GAMMA_FULL * pressure * inverse)
        for r in range(0, rows, 8):
            for z in range(0, width, 128):
                top = jnp.maximum(top, speed[r:r + 8, z:z + 128])
        return top

    best[0] = lax.fori_loop(0, layers, speed_step, jnp.zeros((8, 128), jnp.float32))

    pl.semaphore_wait(barrier, len(others))

    def remote(src, dst, send, recv, where):
        return pltpu.make_async_remote_copy(
            src_ref=src, dst_ref=dst, send_sem=send, recv_sem=recv,
            device_id=where, device_id_type=MESH)

    own = (half * parity, half - half * parity)
    seen = (half - half * parity, half * parity)
    x_out, x_in = 2 * layers * parity, 2 * layers * (1 - parity)
    z_out = z_in = 2 * layers * parity
    pieces = [(h, c) for h in range(2) for c in (0, 1, 2, 3, 4, -1)]
    x_sends, x_waits, z_sends, z_waits = [], [], [], []
    for k, (h, c) in enumerate(pieces):
        def x_copy(start, where):
            if c < 0:
                return remote(
                    mask_own.at[pl.ds(start, half)],
                    mask.at[pl.ds(where + start, half), lo:hi, :],
                    sx.at[k], rx.at[k], {"gx": partner})
            return remote(
                q_own.at[c, pl.ds(start, half)],
                state.at[c, pl.ds(where + start, half), lo:hi, :],
                sx.at[k], rx.at[k], {"gx": partner})

        def z_copy(start, source, target):
            if c < 0:
                return remote(
                    mask.at[pl.ds(source + start, half), lo:hi, :],
                    mask.at[pl.ds(target + start, half), lo:hi, :],
                    sz.at[k], rz.at[k], {"gx": z_to})
            return remote(
                state.at[c, pl.ds(source + start, half), lo:hi, :],
                state.at[c, pl.ds(target + start, half), lo:hi, :],
                sz.at[k], rz.at[k], {"gx": z_to})

        x_sends.append(x_copy(own[h], x_out))
        x_waits.append(x_copy(seen[h], x_in))
        if c < 0 and h == 1:
            z_sends.append(None)
            z_waits.append(None)
        else:
            z_sends.append(z_copy(seen[h], x_in, z_out))
            z_waits.append(z_copy(seen[h], z_in, z_in))

    def max_copy(k):
        source = 0 if k < 3 else 4
        return remote(best.at[source], best.at[k + 1 if k < 3 else k + 2],
                      sm.at[k], rm.at[k], others[k])

    max_copies = [max_copy(k) for k in range(len(others))]
    for copy in max_copies[:3]:
        copy.start()

    for copy in x_sends[:AHEAD]:
        copy.start()

    to_sibling = {"gy": sibling}
    edges = [
        remote(q_own.at[:, :, 0:EDGE, :], state.at[:, layers:2 * layers, hi:tall, :],
               sy.at[0], ry.at[0], to_sibling),
        remote(q_own.at[:, :, rows - EDGE:rows, :], state.at[:, layers:2 * layers, 0:lo, :],
               sy.at[1], ry.at[1], to_sibling),
        remote(mask_own.at[:, 0:EDGE, :], mask.at[layers:2 * layers, hi:tall, :],
               sy.at[2], ry.at[2], to_sibling),
        remote(mask_own.at[:, rows - EDGE:rows, :], mask.at[layers:2 * layers, 0:lo, :],
               sy.at[3], ry.at[3], to_sibling),
    ]

    def corner(where, k):
        spot = pl.ds(where, half)
        return [
            remote(state.at[:, spot, lo:lo + EDGE, :], state.at[:, spot, hi:tall, :],
                   sy.at[k], ry.at[k], to_sibling),
            remote(state.at[:, spot, hi - EDGE:hi, :], state.at[:, spot, 0:lo, :],
                   sy.at[k + 1], ry.at[k + 1], to_sibling),
        ]

    corner_z = corner(z_in + seen[0], 4)
    corner_x = corner(x_in + seen[1], 6)
    for copy in edges:
        copy.start()
    z_inner, z_outer = z_in + seen[0], z_in + seen[1]
    x_outer, x_inner = x_in + seen[0], x_in + seen[1]
    own_z = layers + half * parity
    own_x = layers + half * (1 - parity)

    def each(start, count, body):
        def step(t, carry):
            body(start + t)
            return carry
        lax.fori_loop(0, count, step, 0)

    def store_flux(source, first, last):
        target = fluxes if source is state else fluxes_two

        def store(l):
            _, momenta, energy, inverse, _, pressure = primitives(
                lambda c: source[c, l, first:last, :])
            parts = flux(momenta, energy, inverse, pressure, 0)
            for c in range(1, 5):
                target[c - 1, l, first:last, :] = parts[c]
        return store

    def store_part(source, first, last):
        inner = slice(first, last)

        def store(l):
            _, momenta, energy, inverse, _, pressure = primitives(lambda c: source[c, l])
            fy = flux(momenta, energy, inverse, pressure, 1)
            fz = flux(
                [m[inner] for m in momenta], energy[inner], inverse[inner], pressure[inner], 2)
            for c in range(5):
                q = None if c == 0 else source[c, l]
                total = rolled_terms(fy[c], q, 0)[inner]
                if c == 0:
                    total = total + rolled_terms(fz[c], None, 1)
                else:
                    total = total + rolled_terms(fz[c], q[inner], 1)
                    total = total - (90.0 * VISCOSITY) * q[inner]
                part[c, l, first:last, :] = total
        return store

    def whole(source, c, l, first, last):
        at = lambda ref, index, d: ref[index, l + d, first:last, :]
        x_flux = fluxes if source is state else fluxes_two
        f = (lambda d: at(source, 1, d)) if c == 0 else (lambda d: at(x_flux, c - 1, d))
        total = part[c, l, first:last, :] + 8.0 * (f(-1) - f(1)) - (f(-2) - f(2))
        if c > 0:
            q = lambda d: at(source, c, d)
            total = total + VISCOSITY * (16.0 * (q(-1) + q(1)) - (q(-2) + q(2)))
        return total

    def damping(l, first, last, time_step):
        brinkman = mask[l, first:last, :].astype(jnp.float32) * penalty[...]
        return 1.0 / (1.0 + time_step * brinkman)

    def section_one(first, last, time_step):
        scale = time_step / 12.0

        def body(l):
            damp = damping(l, first, last, time_step)
            for c in range(5):
                value = state[c, l, first:last, :] + scale * whole(state, c, l, first, last)
                stage[c, l, first:last, :] = value * damp if 1 <= c <= 3 else value
        return body

    for k in range(len(pieces)):
        x_waits[k].wait_recv()
        if z_sends[k] is not None:
            z_sends[k].start()
        if k + AHEAD < len(pieces):
            x_sends[k + AHEAD].start()
        if k == 0:
            for copy in edges:
                copy.wait_recv()
            local_q.wait()
            each(own_z, half, store_part(state, 0, tall))
        if k == 1:
            for copy in max_copies[:3]:
                copy.wait_recv()
            best[4] = jnp.maximum(
                jnp.maximum(best[0], best[1]), jnp.maximum(best[2], best[3]))
            for copy in max_copies[3:]:
                copy.start()
            each(own_x, half, store_part(state, 0, tall))
        if k == 2:
            each(layers, layers, store_flux(state, 0, tall))
        if k == 5:
            each(x_outer, half, store_flux(state, lo, hi))
        if k == 6:
            for h in range(5):
                z_waits[h].wait_recv()
            for copy in corner_z:
                copy.start()
        if k == 7:
            for copy in corner_z:
                copy.wait_recv()
            each(z_inner, half, store_flux(state, 0, tall))
            each(z_inner, half, store_part(state, lo, hi))
        if k == 8:
            for copy in max_copies[3:]:
                copy.wait_recv()
            local_m.wait()
            top = best[4]
            for m in range(len(level)):
                top = jnp.maximum(top, best[5 + m])
            top = jnp.max(jnp.max(top, axis=1, keepdims=True), axis=0, keepdims=True)
            time_step = COURANT / top
            each(own_z, half, section_one(0, tall, time_step))
        if k == 9:
            each(own_z, half, store_part(stage, lo, hi))
            each(own_z, half, store_flux(stage, lo, hi))
        if k == 10:
            for copy in corner_x:
                copy.start()
            each(x_inner, half, store_flux(state, lo, hi))

    z_waits[5].wait_recv()
    each(own_x, half, section_one(lo, hi, time_step))
    for k in range(6, 11):
        z_waits[k].wait_recv()
    each(z_outer, half, store_flux(state, lo, hi))
    each(z_inner, half, section_one(lo, hi, time_step))
    each(z_inner, half, store_flux(stage, lo, hi))
    for copy in corner_x:
        copy.wait_recv()
    for first, last in ((0, lo), (hi, tall)):
        each(x_inner, half, store_flux(state, first, last))
        each(own_x, half, section_one(first, last, time_step))
    each(x_inner, half, store_part(state, lo, hi))
    each(x_inner, half, section_one(lo, hi, time_step))
    each(x_inner, half, store_flux(stage, lo, hi))
    each(own_x, half, store_part(stage, lo, hi))
    each(own_x, half, store_flux(stage, lo, hi))

    scale = time_step / 12.0

    def section_two(l):
        damp = damping(l, lo, hi, time_step)
        for c in range(5):
            value = 0.5 * state[c, l, lo:hi, :] + 0.5 * (
                stage[c, l, lo:hi, :] + scale * whole(stage, c, l, lo, hi))
            out[c, l - layers] = value * damp if 1 <= c <= 3 else value

    each(layers, layers, section_two)

    for copy in x_sends + edges + corner_x + corner_z + max_copies:
        copy.wait_send()
    for copy in z_sends:
        if copy is not None:
            copy.wait_send()


def per_device(n, conserved, solid_mask, penalty):
    _, layers, rows, width = conserved.shape
    tall = rows + 2 * EDGE
    dma = pltpu.SemaphoreType.DMA
    return pl.pallas_call(
        functools.partial(kernel, n),
        out_shape=jax.ShapeDtypeStruct(conserved.shape, jnp.float32),
        in_specs=[
            pl.BlockSpec(memory_space=pltpu.VMEM),
            pl.BlockSpec(memory_space=pltpu.VMEM),
            pl.BlockSpec(memory_space=pltpu.VMEM),
        ],
        out_specs=pl.BlockSpec(memory_space=pltpu.VMEM),
        scratch_shapes=[
            pltpu.VMEM((5, 3 * layers, tall, width), jnp.float32),
            pltpu.VMEM((3 * layers, tall, width), jnp.int32),
            pltpu.VMEM((4, 3 * layers, tall, width), jnp.float32),
            pltpu.VMEM((4, 3 * layers, tall, width), jnp.float32),
            pltpu.VMEM((5, 3 * layers, tall, width), jnp.float32),
            pltpu.VMEM((5, 3 * layers, tall, width), jnp.float32),
            pltpu.VMEM((n // 2 + 4, 8, 128), jnp.float32),
            dma((2,)),
            dma((12,)), dma((12,)),
            dma((12,)), dma((12,)),
            dma((8,)), dma((8,)),
            dma((n // 2 + 2,)), dma((n // 2 + 2,)),
        ],
        compiler_params=pltpu.CompilerParams(
            collective_id=0, has_side_effects=True, vmem_limit_bytes=40 * 1024 * 1024),
    )(conserved, solid_mask, penalty.reshape(1, width))


def solution(mesh):
    return jax.shard_map(
        functools.partial(per_device, mesh.shape["gx"]),
        mesh=mesh,
        in_specs=(
            P(None, ("member", "gx"), "gy", None),
            P(("member", "gx"), "gy", None),
            P("member"),
        ),
        out_specs=P(None, ("member", "gx"), "gy", None),
        check_vma=False,
    )
```

```python
import functools

import jax
import jax.numpy as jnp
from jax import lax
from jax.experimental import pallas as pl
from jax.experimental.pallas import tpu as pltpu
from jax.sharding import PartitionSpec as P

GAMMA_LESS = 0.4
GAMMA_FULL = 1.4
COURANT = 0.3
VISCOSITY = 0.05
MESH = pl.DeviceIdType.MESH
EDGE = 8
AHEAD = 8
FIRST = 4


def rolled(value, shift, axis):
    return pltpu.roll(value, shift % value.shape[axis], axis)


def primitives(read):
    rho, m0, m1, m2, energy = [read(c) for c in range(5)]
    inverse = 1.0 / rho
    squares = m0 * m0 + m1 * m1 + m2 * m2
    pressure = GAMMA_LESS * (energy - 0.5 * squares * inverse)
    return rho, (m0, m1, m2), energy, inverse, squares, pressure


def flux(momenta, energy, inverse, pressure, k):
    w = momenta[k] * inverse
    parts = [momenta[k]] + [m * w for m in momenta] + [(energy + pressure) * w]
    parts[1 + k] = parts[1 + k] + pressure
    return parts


def rolled_terms(f, q, axis):
    if q is None:
        return (
            8.0 * (rolled(f, 1, axis) - rolled(f, -1, axis))
            - (rolled(f, 2, axis) - rolled(f, -2, axis))
        )
    s = VISCOSITY * q
    big, wide = 8.0 * f, 16.0 * s
    return (
        rolled(wide + big, 1, axis)
        + rolled(wide - big, -1, axis)
        - rolled(s + f, 2, axis)
        - rolled(s - f, -2, axis)
    )


def kernel(n, q_own, mask_own, penalty_own, out, state, mask, penalty, fluxes, fluxes_two, stage, part, best,
           local_sem, sx, rx, sz, rz, sy, ry, sm, rm):
    i = lax.axis_index("gx")
    g = lax.axis_index("gy")
    layers, rows, width = q_own.shape[1:]
    lo, hi, tall = EDGE, EDGE + rows, rows + 2 * EDGE
    half = layers // 2
    parity = lax.rem(i, 2)
    partner = i + 1 - 2 * parity
    sibling = 1 - g
    z_to = lax.rem(i + 2 - 4 * parity + n, n)
    z_from = lax.rem(i - 2 + 4 * parity + n, n)
    level = [lax.rem(i + 2 * m, n) for m in range(1, n // 2)]

    local_q = pltpu.make_async_copy(
        q_own, state.at[:, layers:2 * layers, lo:hi, :], local_sem.at[0])
    local_m = pltpu.make_async_copy(
        mask_own, mask.at[layers:2 * layers, lo:hi, :], local_sem.at[1])
    local_q.start()
    local_m.start()
    local_p = pltpu.make_async_copy(penalty_own, penalty, local_sem.at[2])
    local_p.start()

    barrier = pltpu.get_barrier_semaphore()
    near_by = [{"gy": sibling}, {"gx": partner}, {"gx": partner, "gy": sibling}]
    others = near_by + [{"gx": j} for j in level]
    for where in others:
        pl.semaphore_signal(barrier, inc=1, device_id=where, device_id_type=MESH)
    pl.semaphore_wait(barrier, len(others))

    def remote(src, dst, send, recv, where):
        return pltpu.make_async_remote_copy(
            src_ref=src, dst_ref=dst, send_sem=send, recv_sem=recv,
            device_id=where, device_id_type=MESH)

    own = (half * parity, half - half * parity)
    seen = (half - half * parity, half * parity)
    x_out, x_in = 2 * layers * parity, 2 * layers * (1 - parity)
    z_out = z_in = 2 * layers * parity
    pieces = [(h, c, d) for h in range(2) for c in (0, 1, 2, 3, 4, -1) for d in range(half)]
    x_sends, x_waits, z_sends, z_waits = [], [], [], []
    for k, (h, c, d) in enumerate(pieces):
        def x_copy(start, where):
            if c < 0:
                return remote(
                    mask_own.at[pl.ds(start, 1)],
                    mask.at[pl.ds(where + start, 1), lo:hi, :],
                    sx.at[k], rx.at[k], {"gx": partner})
            return remote(
                q_own.at[c, pl.ds(start, 1)],
                state.at[c, pl.ds(where + start, 1), lo:hi, :],
                sx.at[k], rx.at[k], {"gx": partner})

        def z_copy(start, source, target):
            if c < 0:
                return remote(
                    mask.at[pl.ds(source + start, 1), lo:hi, :],
                    mask.at[pl.ds(target + start, 1), lo:hi, :],
                    sz.at[k], rz.at[k], {"gx": z_to})
            return remote(
                state.at[c, pl.ds(source + start, 1), lo:hi, :],
                state.at[c, pl.ds(target + start, 1), lo:hi, :],
                sz.at[k], rz.at[k], {"gx": z_to})

        x_sends.append(x_copy(own[h] + d, x_out))
        x_waits.append(x_copy(seen[h] + d, x_in))
        if c < 0 and h == 1:
            z_sends.append(None)
            z_waits.append(None)
        else:
            z_sends.append(z_copy(seen[h] + d, x_in, z_out))
            z_waits.append(z_copy(seen[h] + d, z_in, z_in))

    for copy in x_sends[:FIRST]:
        copy.start()

    to_sibling = {"gy": sibling}
    edges = [
        remote(q_own.at[:, :, 0:EDGE, :], state.at[:, layers:2 * layers, hi:tall, :],
               sy.at[0], ry.at[0], to_sibling),
        remote(q_own.at[:, :, rows - EDGE:rows, :], state.at[:, layers:2 * layers, 0:lo, :],
               sy.at[1], ry.at[1], to_sibling),
        remote(mask_own.at[:, 0:EDGE, :], mask.at[layers:2 * layers, hi:tall, :],
               sy.at[2], ry.at[2], to_sibling),
        remote(mask_own.at[:, rows - EDGE:rows, :], mask.at[layers:2 * layers, 0:lo, :],
               sy.at[3], ry.at[3], to_sibling),
    ]

    def corner(where, k):
        spot = pl.ds(where, half)
        return [
            remote(state.at[:, spot, lo:lo + EDGE, :], state.at[:, spot, hi:tall, :],
                   sy.at[k], ry.at[k], to_sibling),
            remote(state.at[:, spot, hi - EDGE:hi, :], state.at[:, spot, 0:lo, :],
                   sy.at[k + 1], ry.at[k + 1], to_sibling),
        ]

    corner_z = corner(z_in + seen[0], 4)
    corner_x = corner(x_in + seen[1], 6)
    for copy in edges:
        copy.start()

    def speed_step(l, top):
        rho, _, _, inverse, squares, pressure = primitives(
            lambda c: state[c, layers + l, lo:hi, :])
        speed = jnp.sqrt(squares * inverse * inverse) + jnp.sqrt(
            GAMMA_FULL * pressure * inverse)
        for r in range(0, rows, 8):
            for z in range(0, width, 128):
                top = jnp.maximum(top, speed[r:r + 8, z:z + 128])
        return top

    local_q.wait()
    best[0] = lax.fori_loop(0, layers, speed_step, jnp.zeros((8, 128), jnp.float32))

    def max_copy(k):
        source = 0 if k < 3 else 4
        return remote(best.at[source], best.at[k + 1 if k < 3 else k + 2],
                      sm.at[k], rm.at[k], others[k])

    max_copies = [max_copy(k) for k in range(len(others))]
    for copy in max_copies[:3]:
        copy.start()

    for copy in x_sends[FIRST:AHEAD]:
        copy.start()

    z_inner, z_outer = z_in + seen[0], z_in + seen[1]
    x_outer, x_inner = x_in + seen[0], x_in + seen[1]
    own_z = layers + half * parity
    own_x = layers + half * (1 - parity)

    def each(start, count, body):
        def step(t, carry):
            body(start + t)
            return carry
        lax.fori_loop(0, count, step, 0)

    def store_flux(source, first, last):
        target = fluxes if source is state else fluxes_two

        def store(l):
            _, momenta, energy, inverse, _, pressure = primitives(
                lambda c: source[c, l, first:last, :])
            parts = flux(momenta, energy, inverse, pressure, 0)
            for c in range(1, 5):
                target[c - 1, l, first:last, :] = parts[c]
        return store

    def store_part(source, first, last):
        inner = slice(first, last)

        def store(l):
            _, momenta, energy, inverse, _, pressure = primitives(lambda c: source[c, l])
            fy = flux(momenta, energy, inverse, pressure, 1)
            fz = flux(
                [m[inner] for m in momenta], energy[inner], inverse[inner], pressure[inner], 2)
            for c in range(5):
                q = None if c == 0 else source[c, l]
                total = rolled_terms(fy[c], q, 0)[inner]
                if c == 0:
                    total = total + rolled_terms(fz[c], None, 1)
                else:
                    total = total + rolled_terms(fz[c], q[inner], 1)
                    total = total - (90.0 * VISCOSITY) * q[inner]
                part[c, l, first:last, :] = total
        return store

    def whole(source, c, l, first, last):
        at = lambda ref, index, d: ref[index, l + d, first:last, :]
        x_flux = fluxes if source is state else fluxes_two
        f = (lambda d: at(source, 1, d)) if c == 0 else (lambda d: at(x_flux, c - 1, d))
        total = part[c, l, first:last, :] + 8.0 * (f(-1) - f(1)) - (f(-2) - f(2))
        if c > 0:
            q = lambda d: at(source, c, d)
            total = total + VISCOSITY * (16.0 * (q(-1) + q(1)) - (q(-2) + q(2)))
        return total

    def damping(l, first, last, time_step):
        brinkman = mask[l, first:last, :].astype(jnp.float32) * penalty[...]
        return 1.0 / (1.0 + time_step * brinkman)

    def section_one(first, last, time_step):
        scale = time_step / 12.0

        def body(l):
            damp = damping(l, first, last, time_step)
            for c in range(5):
                value = state[c, l, first:last, :] + scale * whole(state, c, l, first, last)
                stage[c, l, first:last, :] = value * damp if 1 <= c <= 3 else value
        return body

    for k in range(len(pieces)):
        x_waits[k].wait_recv()
        if z_sends[k] is not None:
            z_sends[k].start()
        if k + AHEAD < len(pieces):
            x_sends[k + AHEAD].start()
        if k == half * 0 + half - 1:
            for copy in edges:
                copy.wait_recv()
            each(own_z, half, store_part(state, 0, tall))
        if k == half * 1 + half - 1:
            for copy in max_copies[:3]:
                copy.wait_recv()
            best[4] = jnp.maximum(
                jnp.maximum(best[0], best[1]), jnp.maximum(best[2], best[3]))
            for copy in max_copies[3:]:
                copy.start()
            each(own_x, half, store_part(state, 0, tall))
        if k == half * 2 + half - 1:
            each(layers, layers, store_flux(state, 0, tall))
        if k == half * 5 + half - 1:
            each(x_outer, half, store_flux(state, lo, hi))
        if k == half * 6 + half - 1:
            for h in range(5 * half):
                z_waits[h].wait_recv()
            for copy in corner_z:
                copy.start()
        if k == half * 7 + half - 1:
            for copy in corner_z:
                copy.wait_recv()
            each(z_inner, half, store_flux(state, 0, tall))
            each(z_inner, half, store_part(state, lo, hi))
        if k == half * 8 + half - 1:
            for copy in max_copies[3:]:
                copy.wait_recv()
            local_m.wait()
            local_p.wait()
            top = best[4]
            for m in range(len(level)):
                top = jnp.maximum(top, best[5 + m])
            top = jnp.max(jnp.max(top, axis=1, keepdims=True), axis=0, keepdims=True)
            time_step = COURANT / top
            each(own_z, half, section_one(0, tall, time_step))
        if k == half * 9 + half - 1:
            each(own_z, half, store_part(stage, lo, hi))
            each(own_z, half, store_flux(stage, lo, hi))
        if k == half * 10 + half - 1:
            for copy in corner_x:
                copy.start()
            each(x_inner, half, store_flux(state, lo, hi))

    for h in range(5 * half, 6 * half):
        z_waits[h].wait_recv()
    each(own_x, half, section_one(lo, hi, time_step))
    for k in range(6 * half, 11 * half):
        z_waits[k].wait_recv()
    each(z_outer, half, store_flux(state, lo, hi))
    each(z_inner, half, section_one(lo, hi, time_step))
    each(z_inner, half, store_flux(stage, lo, hi))
    for copy in corner_x:
        copy.wait_recv()
    for first, last in ((0, lo), (hi, tall)):
        each(x_inner, half, store_flux(state, first, last))
        each(own_x, half, section_one(first, last, time_step))
    each(x_inner, half, store_part(state, lo, hi))
    each(x_inner, half, section_one(lo, hi, time_step))
    each(x_inner, half, store_flux(stage, lo, hi))
    each(own_x, half, store_part(stage, lo, hi))
    each(own_x, half, store_flux(stage, lo, hi))

    scale = time_step / 12.0

    def section_two(l):
        damp = damping(l, lo, hi, time_step)
        for c in range(5):
            value = 0.5 * state[c, l, lo:hi, :] + 0.5 * (
                stage[c, l, lo:hi, :] + scale * whole(stage, c, l, lo, hi))
            out[c, l - layers] = value * damp if 1 <= c <= 3 else value

    each(layers, layers, section_two)

    for copy in x_sends + edges + corner_x + corner_z + max_copies:
        copy.wait_send()
    for copy in z_sends:
        if copy is not None:
            copy.wait_send()


def per_device(n, conserved, solid_mask, penalty):
    _, layers, rows, width = conserved.shape
    tall = rows + 2 * EDGE
    dma = pltpu.SemaphoreType.DMA
    return pl.pallas_call(
        functools.partial(kernel, n),
        out_shape=pltpu.VMEM(conserved.shape, jnp.float32),
        in_specs=[
            pl.BlockSpec(memory_space=pltpu.HBM),
            pl.BlockSpec(memory_space=pltpu.HBM),
            pl.BlockSpec(memory_space=pltpu.HBM),
        ],
        out_specs=pl.BlockSpec(memory_space=pltpu.VMEM),
        scratch_shapes=[
            pltpu.VMEM((5, 3 * layers, tall, width), jnp.float32),
            pltpu.VMEM((3 * layers, tall, width), jnp.int32),
            pltpu.VMEM((1, width), jnp.float32),
            pltpu.VMEM((4, 3 * layers, tall, width), jnp.float32),
            pltpu.VMEM((4, 3 * layers, tall, width), jnp.float32),
            pltpu.VMEM((5, 3 * layers, tall, width), jnp.float32),
            pltpu.VMEM((5, 3 * layers, tall, width), jnp.float32),
            pltpu.VMEM((n // 2 + 4, 8, 128), jnp.float32),
            dma((3,)),
            dma((6 * layers,)), dma((6 * layers,)),
            dma((6 * layers,)), dma((6 * layers,)),
            dma((8,)), dma((8,)),
            dma((n // 2 + 2,)), dma((n // 2 + 2,)),
        ],
        compiler_params=pltpu.CompilerParams(
            collective_id=0, has_side_effects=True, vmem_limit_bytes=63500 * 1024),
    )(conserved, solid_mask, penalty.reshape(1, width))


def solution(mesh):
    return jax.shard_map(
        functools.partial(per_device, mesh.shape["gx"]),
        mesh=mesh,
        in_specs=(
            P(None, ("member", "gx"), "gy", None),
            P(("member", "gx"), "gy", None),
            P("member"),
        ),
        out_specs=P(None, ("member", "gx"), "gy", None),
        check_vma=False,
    )
```
